32 devices in a mesh: dp: 4 (over y, core), expert: 8 (over z, x).
Axes of the slice: x: 2, y: 2, z: 4, core: 2. Of those that a mesh axis runs over, the one named last changes fastest.
Arguments:
- tokens: bfloat16 [6144, 4096], P(('dp', 'expert')), may hold values from -6 to 6
- cotangent: bfloat16 [6144, 4096], P(('dp', 'expert')), may hold values from -6 to 6
- expert_ids: int32 [6144, 6], P(('dp', 'expert')), may hold values from 0 to 63, as said below
- route_weights: float32 [6144, 6], P(('dp', 'expert')), may hold values from 0.05 to 1
- expert_weights: bfloat16 [8, 704, 3, 4096], P('expert'), may hold values from -0.09375 to 0.09375
Outputs:
- input_grad: bfloat16 [6144, 4096], P(('dp', 'expert'))
- route_grad: bfloat16 [6144, 6], P(('dp', 'expert'))
- weight_grad: float32 [8, 704, 3, 4096], P('expert', 'dp')
The draws below stay inside these ranges and needn't reach their ends.
Inputs may be any that keep to these rules, and one draw needn't show every extreme that they name: `expert_ids`: each row names 6 different experts. Only experts below 8 are in this window; in the rows of one device (aligned blocks of 192 rows) each of them is named at most 36 times.
All inputs are finite; a program needn't handle non-finite values.
Results may differ from the reference program's by a relative error of at most 0.015.
Values may be sent and summed in bfloat16 or wider, within the bound.
A program may use at most 128 MiB of HBM per device.

```python
import math
import jax
import jax.numpy as jnp
from jax import lax

D = 4096
HID = 704
EXPERTS = 64
TOP = 6
TOK_DEV = 192
FLIGHT = 8
CAP = 36
TOKENS = 6144
N_DP = 4
N_EXPERT = 8


def draw_expert_ids(key, part):
    base_key = jax.random.fold_in(key, 11)
    block_total = TOKENS // TOK_DEV
    hottest = jax.random.randint(jax.random.fold_in(base_key, 7), (), 0, FLIGHT)
    others = EXPERTS - FLIGHT

    def one_block(block_key):
        load_key, order_key, turn_key = jax.random.split(block_key, 3)
        loads = jax.random.randint(load_key, (FLIGHT,), 0, CAP + 1)
        loads = jnp.where(jnp.arange(FLIGHT) == hottest, CAP, loads)
        remain = TOK_DEV * TOP - jnp.sum(loads)
        spare_index = jnp.arange(others)
        spare_loads = remain // others + (spare_index < remain % others).astype(jnp.int32)
        counts = jnp.concatenate([loads, spare_loads]).astype(jnp.int32)
        deck = jnp.repeat(jnp.arange(EXPERTS, dtype=jnp.int32), counts, total_repeat_length=TOK_DEV * TOP)
        dealt = deck.reshape(TOP, TOK_DEV).T
        order = jax.random.permutation(order_key, TOK_DEV)
        dealt = dealt[order]
        turns = jax.random.randint(turn_key, (TOK_DEV, 1), 0, TOP)
        columns = (jnp.arange(TOP)[None, :] + turns) % TOP
        return jnp.take_along_axis(dealt, columns, axis=1)
    block_keys = jax.random.split(base_key, block_total)
    return jax.vmap(one_block)(block_keys).reshape(TOKENS, TOP).astype(jnp.int32)


def block_levels(key, dims, shards, low, largest):
    loudness, own = 1.0, jax.random.fold_in(key, 6)
    for axis_at, blocks in shards:
        heights = jnp.exp(jax.random.uniform(jax.random.fold_in(own, axis_at), (blocks,), jnp.float32, low / len(shards), largest / len(shards)))
        loudness = loudness * jnp.repeat(heights, dims[axis_at] // blocks).reshape([-1 if axis == axis_at else 1 for axis in range(len(dims))])
    return loudness


def normal_values(key, extent, width, limit, shards=(), kind=jnp.bfloat16):
    drawn = width * jax.random.normal(key, extent, jnp.float32)
    if shards:
        drawn = drawn * block_levels(key, extent, shards, -0.22, 0.18)
    return jnp.clip(drawn, -limit, limit).astype(kind)


def setup_inputs(seed: int = 0) -> dict:
    key_list = jax.random.split(jax.random.key(seed), 6)
    return {
        "tokens": normal_values(key_list[0], (TOKENS, D), 1.0, 6.0, ((0, 32),)),
        "cotangent": normal_values(key_list[1], (TOKENS, D), 1.0, 6.0, ((0, 32),)),
        "expert_ids": draw_expert_ids(jax.random.fold_in(key_list[5], 71), 0),
        "route_weights": jnp.clip(jnp.exp(math.log(1.0) - 2.9957323 * jax.random.uniform(key_list[3], (TOKENS, TOP), jnp.float32) ** block_levels(key_list[3], (TOKENS, TOP), ((0, 32),), -0.2, 0.2)), 0.05, 1.0),
        "expert_weights": normal_values(key_list[4], (FLIGHT, HID, 3, D), D ** -0.5, 0.09375, ((0, 8),)),
    }


def expert_pass(token_rows, cot_rows, row_scale, weights):
    weights32 = weights.astype(jnp.float32)
    token32 = token_rows.astype(jnp.float32)
    cot32 = cot_rows.astype(jnp.float32)
    gate_pre = jnp.einsum("md,hd->mh", token32, weights32[:, 0, :])
    up_pre = jnp.einsum("md,hd->mh", token32, weights32[:, 1, :])
    logistic = jax.nn.sigmoid(gate_pre)
    hidden = (gate_pre * logistic * up_pre).astype(jnp.bfloat16)
    back_proj = jnp.einsum("md,hd->mh", cot32, weights32[:, 2, :])
    route_rows = jnp.sum(hidden.astype(jnp.float32) * back_proj, axis=1).astype(jnp.bfloat16)
    scale32 = row_scale.astype(jnp.float32)[:, None]
    scaled = (scale32 * cot32).astype(jnp.bfloat16)
    grad_hidden = scale32 * back_proj
    gate_delta = (grad_hidden * up_pre * logistic * (1.0 + gate_pre * (1.0 - logistic))).astype(jnp.bfloat16)
    up_delta = (grad_hidden * gate_pre * logistic).astype(jnp.bfloat16)
    gd32 = gate_delta.astype(jnp.float32)
    ud32 = up_delta.astype(jnp.float32)
    input_rows = (jnp.einsum("mh,hd->md", gd32, weights32[:, 0, :]) + jnp.einsum("mh,hd->md", ud32, weights32[:, 1, :])).astype(jnp.bfloat16)
    gate_term = jnp.einsum("mh,md->hd", gd32, token32)
    up_term = jnp.einsum("mh,md->hd", ud32, token32)
    down_term = jnp.einsum("mh,md->hd", hidden.astype(jnp.float32), scaled.astype(jnp.float32))
    term = jnp.stack([gate_term, up_term, down_term], axis=1)
    return input_rows, route_rows, term


def reference(tokens, cotangent, expert_ids, route_weights, expert_weights):
    group_rows = TOK_DEV * N_EXPERT
    route_count = group_rows * TOP
    slot_count = N_EXPERT * CAP

    def per_group(weight_acc, group_index):
        first_row = (group_index * group_rows).astype(jnp.int32)
        group_tokens = lax.dynamic_slice_in_dim(tokens, first_row, group_rows, 0)
        group_cot = lax.dynamic_slice_in_dim(cotangent, first_row, group_rows, 0)
        group_ids = lax.dynamic_slice_in_dim(expert_ids, first_row, group_rows, 0).reshape(-1)
        group_scale = lax.dynamic_slice_in_dim(route_weights, first_row, group_rows, 0).reshape(-1)

        def per_expert(carry, expert_index):
            input_acc, route_acc, weight_now = carry
            chosen = jnp.nonzero(group_ids == expert_index, size=slot_count, fill_value=route_count)[0].astype(jnp.int32)
            filled = chosen < route_count
            safe_index = jnp.minimum(chosen, route_count - 1)
            owner_row = safe_index // TOP
            zero16 = jnp.zeros((), jnp.bfloat16)
            token_rows = jnp.where(filled[:, None], group_tokens[owner_row], zero16)
            cot_rows = jnp.where(filled[:, None], group_cot[owner_row], zero16)
            row_scale = jnp.where(filled, group_scale[safe_index], jnp.float32(0.0)).astype(jnp.bfloat16)
            weights = lax.dynamic_index_in_dim(expert_weights, expert_index, 0, keepdims=False)
            input_rows, route_rows, term = expert_pass(token_rows, cot_rows, row_scale, weights)
            rounded = lax.optimization_barrier(term.astype(jnp.bfloat16)).astype(jnp.float32)
            weight_now = weight_now.at[expert_index].add(rounded)
            input_acc = input_acc.at[owner_row].add(jnp.where(filled[:, None], input_rows.astype(jnp.float32), jnp.float32(0.0)))
            route_acc = route_acc.at[safe_index].add(jnp.where(filled, route_rows.astype(jnp.float32), jnp.float32(0.0)))
            return (input_acc, route_acc, weight_now), None

        start = (jnp.zeros((group_rows, D), jnp.float32), jnp.zeros((route_count,), jnp.float32), weight_acc)
        finish, _ = lax.scan(per_expert, start, jnp.arange(FLIGHT, dtype=jnp.int32))
        input_acc, route_acc, weight_acc = finish
        return weight_acc, (input_acc.astype(jnp.bfloat16), route_acc.astype(jnp.bfloat16).reshape(group_rows, TOP))

    weight_start = jnp.zeros((FLIGHT, HID, 3, D), jnp.float32)
    weight_grad, outputs = lax.scan(per_group, weight_start, jnp.arange(N_DP, dtype=jnp.int32))
    input_grad = outputs[0].reshape(TOKENS, D)
    route_grad = outputs[1].reshape(TOKENS, TOP)
    return input_grad, route_grad, weight_grad
```

```python
import functools

import jax
import jax.numpy as jnp
from jax import lax
from jax.experimental import pallas as pl
from jax.experimental.pallas import tpu as pltpu
from jax.sharding import PartitionSpec as P

CAP = 36
MESH = pl.DeviceIdType.MESH
F32 = jnp.float32
BF16 = jnp.bfloat16


def dispatch_kernel(
    n_dp, n_ex, send_ref, out_ref, self_sem, s_ex, r_ex, s_mate, r_mate, s_y, r_y, s_fwd, r_fwd
):
    d, e = lax.axis_index("dp"), lax.axis_index("expert")
    n_y = n_dp // 2
    y, core = d // 2, lax.rem(d, 2)
    mate = d + 1 - 2 * core

    def y_peer(j):
        return lax.rem(y + j, n_y) * 2 + core

    barrier = pltpu.get_barrier_semaphore()
    for k in range(1, n_ex):
        pl.semaphore_signal(barrier, inc=1, device_id=(d, lax.rem(e + k, n_ex)), device_id_type=MESH)
    for j in range(1, n_y):
        pl.semaphore_signal(barrier, inc=1, device_id=(y_peer(j), e), device_id_type=MESH)
    pl.semaphore_signal(barrier, inc=1, device_id=(mate, e), device_id_type=MESH)
    pl.semaphore_wait(barrier, n_ex - 1 + n_y - 1 + 1)

    def source(k):
        return lax.rem(e + n_ex - k, n_ex)

    def to_expert(k):
        dest = lax.rem(e + k, n_ex)
        return pltpu.make_async_remote_copy(
            src_ref=send_ref.at[dest], dst_ref=out_ref.at[d, e], send_sem=s_ex.at[k], recv_sem=r_ex.at[k],
            device_id=(d, dest), device_id_type=MESH)

    def from_expert(k):
        return pltpu.make_async_remote_copy(
            src_ref=send_ref.at[source(k)], dst_ref=out_ref.at[d, source(k)], send_sem=s_ex.at[k],
            recv_sem=r_ex.at[k], device_id=(d, source(k)), device_id_type=MESH)

    def move(group, k, to, send_sem, recv_sem):
        slab = out_ref.at[group, source(k)]
        return pltpu.make_async_remote_copy(
            src_ref=slab, dst_ref=slab, send_sem=send_sem, recv_sem=recv_sem, device_id=(to, e),
            device_id_type=MESH)

    near = sorted(range(1, n_ex), key=lambda k: (min(k, n_ex - k), k))
    far = near[::-1]
    order = []
    for a, b in zip(far, near):
        for k in (a, b):
            if k not in order:
                order.append(k)
    own = pltpu.make_async_copy(send_ref.at[e], out_ref.at[d, e], self_sem)
    own.start()
    for k in order:
        to_expert(k).start()

    arrivals = [0] + near

    def relay(k):
        for j in range(1, n_y):
            group = lax.rem(y + n_y - j, n_y) * 2 + core
            move(group, k, mate, s_y.at[j, k], r_y.at[j, k]).wait_recv()
            move(group, k, mate, s_fwd.at[j, k], r_fwd.at[j, k]).start()

    for i, k in enumerate(arrivals):
        if k == 0:
            own.wait()
        else:
            from_expert(k).wait_recv()
        for j in range(1, n_y):
            move(d, k, y_peer(j), s_y.at[j, k], r_y.at[j, k]).start()
        move(d, k, mate, s_mate.at[k], r_mate.at[k]).start()
        if i >= 2:
            relay(arrivals[i - 2])
    for k in arrivals[-2:]:
        relay(k)
    for k in arrivals:
        move(mate, k, mate, s_mate.at[k], r_mate.at[k]).wait_recv()
        for j in range(1, n_y):
            group = lax.rem(y + n_y - j, n_y) * 2 + 1 - core
            move(group, k, mate, s_fwd.at[j, k], r_fwd.at[j, k]).wait_recv()
    for k in arrivals:
        if k:
            to_expert(k).wait_send()
        move(d, k, mate, s_mate.at[k], r_mate.at[k]).wait_send()
        for j in range(1, n_y):
            move(d, k, y_peer(j), s_y.at[j, k], r_y.at[j, k]).wait_send()
            group = lax.rem(y + n_y - j, n_y) * 2 + core
            move(group, k, mate, s_fwd.at[j, k], r_fwd.at[j, k]).wait_send()


def dispatch(send, n_dp, n_ex):
    _, rows, width = send.shape
    n_y = n_dp // 2
    dma = pltpu.SemaphoreType.DMA
    return pl.pallas_call(
        functools.partial(dispatch_kernel, n_dp, n_ex),
        out_shape=jax.ShapeDtypeStruct((n_dp, n_ex, rows, width), send.dtype),
        in_specs=[pl.BlockSpec(memory_space=pl.ANY)],
        out_specs=pl.BlockSpec(memory_space=pl.ANY),
        scratch_shapes=[
            dma, dma((n_ex,)), dma((n_ex,)), dma((n_ex,)), dma((n_ex,)),
            dma((n_y, n_ex)), dma((n_y, n_ex)), dma((n_y, n_ex)), dma((n_y, n_ex)),
        ],
        compiler_params=pltpu.CompilerParams(collective_id=0, has_side_effects=True),
    )(send)


def activations(pre_tok, pre_cot, hid):
    gate_pre, up_pre = pre_tok[..., :hid], pre_tok[..., hid : 2 * hid]
    grad_hidden = pre_cot[..., 2 * hid :]
    logistic = jax.nn.sigmoid(gate_pre)
    hidden = (gate_pre * logistic * up_pre).astype(BF16)
    gate_delta = (grad_hidden * up_pre * logistic * (1.0 + gate_pre * (1.0 - logistic))).astype(BF16)
    up_delta = (grad_hidden * gate_pre * logistic).astype(BF16)
    return hidden, grad_hidden, gate_delta, up_delta


def shards(tokens, cotangent, expert_ids, route_weights, expert_weights):
    n_ex, n_dp = lax.axis_size("expert"), lax.axis_size("dp")
    tok_rows, width = tokens.shape
    hid = expert_weights.shape[1]
    part = hid // n_dp
    slab = 2 * CAP
    half = width // 2

    columns = jnp.arange(n_ex, dtype=jnp.int32)
    chosen = expert_ids[:, :, None] == columns
    member = jnp.any(chosen, axis=1)
    scale16 = route_weights.astype(BF16).astype(F32)
    scale_te = jnp.sum(jnp.where(chosen, scale16[:, :, None], 0.0), axis=1)
    lower = (jnp.arange(tok_rows)[:, None] > jnp.arange(tok_rows)[None, :]).astype(BF16)
    slot_te = jnp.dot(lower, member.astype(BF16), preferred_element_type=F32).astype(jnp.int32)
    slot = jnp.where(member, slot_te, -1).T
    lanes = jnp.arange(slab, dtype=jnp.int32)[None, :, None]
    pick_tok = (slot[:, None, :] == lanes)
    pick_cot = (slot[:, None, :] == lanes - CAP) & (lanes >= CAP)
    pick_tok = pick_tok & (lanes < CAP)
    row_scale = jnp.sum(jnp.where(pick_cot, scale_te.T[:, None, :], 0.0), axis=2).reshape(-1, 1)
    pick_tok16 = pick_tok.astype(BF16).reshape(-1, tok_rows)
    pick_cot16 = pick_cot.astype(BF16).reshape(-1, tok_rows)
    send = (
        jnp.dot(pick_tok16, tokens, preferred_element_type=F32)
        + row_scale * jnp.dot(pick_cot16, cotangent, preferred_element_type=F32)
    ).astype(BF16)

    rows = dispatch(send.reshape(n_ex, slab, width), n_dp, n_ex)
    d = lax.axis_index("dp")
    weights = jnp.transpose(expert_weights[0], (1, 0, 2))
    flat_weights = weights.reshape(3 * hid, width)

    mine = lax.dynamic_index_in_dim(rows, d, 0, keepdims=False).reshape(n_ex * slab, width)
    pre = lax.dot_general(mine, flat_weights, (((1,), (1,)), ((), ())), preferred_element_type=F32)
    pre = pre.reshape(n_ex, slab, 3 * hid)
    hidden, grad_hidden, gate_delta, up_delta = activations(pre[:, :CAP], pre[:, CAP:], hid)
    route_rows = jnp.sum(hidden.astype(F32) * grad_hidden, axis=2)
    deltas = jnp.concatenate([gate_delta, up_delta], axis=2)
    nothing = jnp.zeros_like(deltas)
    left = jnp.concatenate([deltas, nothing], axis=1).reshape(n_ex * slab, 2 * hid)
    right = jnp.concatenate([nothing, deltas], axis=1).reshape(n_ex * slab, 2 * hid)
    input_rows = (
        jnp.dot(left, flat_weights[: 2 * hid, :half], preferred_element_type=F32)
        + jnp.dot(right, flat_weights[: 2 * hid, half:], preferred_element_type=F32)
    ).astype(BF16)
    back = lax.all_to_all(
        input_rows.reshape(n_ex, slab, half), "expert", split_axis=0, concat_axis=0, tiled=True
    )
    back_route = lax.all_to_all(route_rows, "expert", split_axis=0, concat_axis=0, tiled=True)

    own_weights = lax.dynamic_slice_in_dim(weights, d * part, part, axis=1).reshape(3 * part, width)
    every = rows.reshape(n_dp * n_ex * slab, width)
    pre_all = lax.dot_general(every, own_weights, (((1,), (1,)), ((), ())), preferred_element_type=F32)
    pre_all = pre_all.reshape(n_dp * n_ex, slab, 3 * part)
    hidden_a, _, gate_a, up_a = activations(pre_all[:, :CAP], pre_all[:, CAP:], part)
    top = jnp.concatenate([gate_a, up_a, jnp.zeros_like(hidden_a)], axis=2)
    bottom = jnp.concatenate([jnp.zeros_like(gate_a), jnp.zeros_like(up_a), hidden_a], axis=2)
    factors = jnp.concatenate([top, bottom], axis=1).reshape(-1, 3 * part)
    weight_grad = lax.dot_general(factors, every, (((0,), (0,)), ((), ())), preferred_element_type=F32)
    weight_grad = jnp.transpose(weight_grad.reshape(3, part, width), (1, 0, 2))

    back = back.reshape(n_ex * slab, half)
    input_grad = jnp.concatenate(
        [
            lax.dot_general(p, back, (((0,), (0,)), ((), ())), preferred_element_type=F32).astype(BF16)
            for p in (pick_tok16, pick_cot16)
        ],
        axis=1,
    )
    route_te = jnp.sum(jnp.where(pick_tok[:, :CAP], back_route[:, :, None], 0.0), axis=1).T
    route_grad = (
        jnp.sum(jnp.where(chosen, route_te[:, None, :], 0.0), axis=2) / scale16
    ).astype(BF16)
    return (input_grad, route_grad, weight_grad[None])


def solution(mesh):
    in_specs = (
        P(("dp", "expert"), None),
        P(("dp", "expert"), None),
        P(("dp", "expert"), None),
        P(("dp", "expert"), None),
        P("expert", None, None, None),
    )
    out_specs = (
        P(("dp", "expert"), None),
        P(("dp", "expert"), None),
        P("expert", "dp", None, None),
    )
    return jax.shard_map(shards, mesh=mesh, in_specs=in_specs, out_specs=out_specs, check_vma=False)
```

```python
import functools

import jax
import jax.numpy as jnp
from jax import lax
from jax.experimental import pallas as pl
from jax.experimental.pallas import tpu as pltpu
from jax.sharding import PartitionSpec as P

CAP = 36
MESH = pl.DeviceIdType.MESH
F32 = jnp.float32
BF16 = jnp.bfloat16


def dispatch_kernel(
    n_dp, n_ex, send_ref, out_ref, self_sem, s_ex, r_ex, s_mate, r_mate, s_y, r_y, s_fwd, r_fwd
):
    d, e = lax.axis_index("dp"), lax.axis_index("expert")
    n_y, half = n_dp // 2, n_ex // 2
    y, core = d // 2, lax.rem(d, 2)
    mate = d + 1 - 2 * core
    side, place = e // half, lax.rem(e, half)

    def y_peer(j):
        return lax.rem(y + j, n_y) * 2 + core

    barrier = pltpu.get_barrier_semaphore()
    for k in range(1, n_ex):
        pl.semaphore_signal(barrier, inc=1, device_id=(d, lax.rem(e + k, n_ex)), device_id_type=MESH)
    for j in range(1, n_y):
        pl.semaphore_signal(barrier, inc=1, device_id=(y_peer(j), e), device_id_type=MESH)
    pl.semaphore_signal(barrier, inc=1, device_id=(mate, e), device_id_type=MESH)
    pl.semaphore_wait(barrier, n_ex - 1 + n_y - 1 + 1)

    def across(far):
        return (1 - side) * half if far else side * half

    def to_expert(far, r):
        dest = across(far) + lax.rem(place + r, half)
        return pltpu.make_async_remote_copy(
            src_ref=send_ref.at[dest], dst_ref=out_ref.at[d, e], send_sem=s_ex.at[far, r],
            recv_sem=r_ex.at[far, r], device_id=(d, dest), device_id_type=MESH)

    def source(far, r):
        return across(far) + lax.rem(place + half - r, half)

    def from_expert(far, r):
        src = source(far, r)
        return pltpu.make_async_remote_copy(
            src_ref=send_ref.at[src], dst_ref=out_ref.at[d, src], send_sem=s_ex.at[far, r],
            recv_sem=r_ex.at[far, r], device_id=(d, src), device_id_type=MESH)

    def move(group, far, r, to, send_sem, recv_sem):
        slab = out_ref.at[group, source(far, r)]
        return pltpu.make_async_remote_copy(
            src_ref=slab, dst_ref=slab, send_sem=send_sem, recv_sem=recv_sem, device_id=(to, e),
            device_id_type=MESH)

    def to_mate(group, far, r):
        return move(group, far, r, mate, s_mate.at[far, r], r_mate.at[far, r])

    def to_y(group, far, r, j):
        return move(group, far, r, y_peer(j), s_y.at[j, far, r], r_y.at[j, far, r])

    def pass_on(group, far, r, j):
        return move(group, far, r, mate, s_fwd.at[j, far, r], r_fwd.at[j, far, r])

    def y_source(j):
        return lax.rem(y + n_y - j, n_y) * 2

    def forward(far, r):
        if not far and r == 0:
            own.wait()
        else:
            from_expert(far, r).wait_recv()
        for j in range(1, n_y):
            to_y(d, far, r, j).start()
        to_mate(d, far, r).start()

    def relay(far, r):
        for j in range(1, n_y):
            to_y(y_source(j) + core, far, r, j).wait_recv()
            pass_on(y_source(j) + core, far, r, j).start()

    own = pltpu.make_async_copy(send_ref.at[e], out_ref.at[d, e], self_sem)
    own.start()
    pending = []
    for r in range(half):
        if r:
            to_expert(1, r - 1).wait_send()
        to_expert(1, r).start()
        if r + 1 < half:
            to_expert(0, r + 1).start()
        if r:
            forward(1, r - 1)
            pending.append((1, r - 1))
        forward(0, r)
        pending.append((0, r))
        while len(pending) > 4:
            relay(*pending.pop(0))
    forward(1, half - 1)
    pending.append((1, half - 1))
    for flow in pending:
        relay(*flow)
    flows = [(far, r) for r in range(half) for far in (0, 1)]
    for flow in flows:
        to_mate(mate, *flow).wait_recv()
        for j in range(1, n_y):
            pass_on(y_source(j) + 1 - core, *flow, j).wait_recv()
    to_expert(1, half - 1).wait_send()
    for far, r in flows:
        if not far and r:
            to_expert(far, r).wait_send()
        to_mate(d, far, r).wait_send()
        for j in range(1, n_y):
            to_y(d, far, r, j).wait_send()
            pass_on(y_source(j) + core, far, r, j).wait_send()


def dispatch(send, n_dp, n_ex):
    _, rows, width = send.shape
    n_y, half = n_dp // 2, n_ex // 2
    dma = pltpu.SemaphoreType.DMA
    return pl.pallas_call(
        functools.partial(dispatch_kernel, n_dp, n_ex),
        out_shape=jax.ShapeDtypeStruct((n_dp, n_ex, rows, width), send.dtype),
        in_specs=[pl.BlockSpec(memory_space=pl.ANY)],
        out_specs=pl.BlockSpec(memory_space=pl.ANY),
        scratch_shapes=[
            dma, dma((2, half)), dma((2, half)), dma((2, half)), dma((2, half)),
            dma((n_y, 2, half)), dma((n_y, 2, half)), dma((n_y, 2, half)), dma((n_y, 2, half)),
        ],
        compiler_params=pltpu.CompilerParams(collective_id=0, has_side_effects=True),
    )(send)


def activations(pre_tok, pre_cot, hid):
    gate_pre, up_pre = pre_tok[..., :hid], pre_tok[..., hid : 2 * hid]
    grad_hidden = pre_cot[..., 2 * hid :]
    logistic = jax.nn.sigmoid(gate_pre)
    hidden = (gate_pre * logistic * up_pre).astype(BF16)
    gate_delta = (grad_hidden * up_pre * logistic * (1.0 + gate_pre * (1.0 - logistic))).astype(BF16)
    up_delta = (grad_hidden * gate_pre * logistic).astype(BF16)
    return hidden, grad_hidden, gate_delta, up_delta


def shards(tokens, cotangent, expert_ids, route_weights, expert_weights):
    n_ex, n_dp = lax.axis_size("expert"), lax.axis_size("dp")
    tok_rows, width = tokens.shape
    hid = expert_weights.shape[1]
    part = hid // n_dp
    slab = 2 * CAP
    half = width // 2

    columns = jnp.arange(n_ex, dtype=jnp.int32)
    chosen = expert_ids[:, :, None] == columns
    member = jnp.any(chosen, axis=1)
    scale16 = route_weights.astype(BF16).astype(F32)
    scale_te = jnp.sum(jnp.where(chosen, scale16[:, :, None], 0.0), axis=1)
    lower = (jnp.arange(tok_rows)[:, None] > jnp.arange(tok_rows)[None, :]).astype(BF16)
    slot_te = jnp.dot(lower, member.astype(BF16), preferred_element_type=F32).astype(jnp.int32)
    slot = jnp.where(member, slot_te, -1).T
    lanes = jnp.arange(slab, dtype=jnp.int32)[None, :, None]
    pick_tok = (slot[:, None, :] == lanes)
    pick_cot = (slot[:, None, :] == lanes - CAP) & (lanes >= CAP)
    pick_tok = pick_tok & (lanes < CAP)
    row_scale = jnp.sum(jnp.where(pick_cot, scale_te.T[:, None, :], 0.0), axis=2).reshape(-1, 1)
    pick_tok16 = pick_tok.astype(BF16).reshape(-1, tok_rows)
    pick_cot16 = pick_cot.astype(BF16).reshape(-1, tok_rows)
    send = (
        jnp.dot(pick_tok16, tokens, preferred_element_type=F32)
        + row_scale * jnp.dot(pick_cot16, cotangent, preferred_element_type=F32)
    ).astype(BF16)

    rows = dispatch(send.reshape(n_ex, slab, width), n_dp, n_ex)
    d = lax.axis_index("dp")
    weights = jnp.transpose(expert_weights[0], (1, 0, 2))
    flat_weights = weights.reshape(3 * hid, width)

    mine = lax.dynamic_index_in_dim(rows, d, 0, keepdims=False).reshape(n_ex * slab, width)
    pre = lax.dot_general(mine, flat_weights, (((1,), (1,)), ((), ())), preferred_element_type=F32)
    pre = pre.reshape(n_ex, slab, 3 * hid)
    hidden, grad_hidden, gate_delta, up_delta = activations(pre[:, :CAP], pre[:, CAP:], hid)
    route_rows = jnp.sum(hidden.astype(F32) * grad_hidden, axis=2)
    deltas = jnp.concatenate([gate_delta, up_delta], axis=2)
    nothing = jnp.zeros_like(deltas)
    left = jnp.concatenate([deltas, nothing], axis=1).reshape(n_ex * slab, 2 * hid)
    right = jnp.concatenate([nothing, deltas], axis=1).reshape(n_ex * slab, 2 * hid)
    input_rows = (
        jnp.dot(left, flat_weights[: 2 * hid, :half], preferred_element_type=F32)
        + jnp.dot(right, flat_weights[: 2 * hid, half:], preferred_element_type=F32)
    ).astype(BF16)
    back = lax.all_to_all(
        input_rows.reshape(n_ex, slab, half), "expert", split_axis=0, concat_axis=0, tiled=True
    )
    all_route = lax.all_gather(route_rows, "expert", axis=0, tiled=False)
    back_route = lax.dynamic_index_in_dim(all_route, lax.axis_index("expert"), 1, keepdims=False)

    own_weights = lax.dynamic_slice_in_dim(weights, d * part, part, axis=1).reshape(3 * part, width)
    every = rows.reshape(n_dp * n_ex * slab, width)
    pre_all = lax.dot_general(every, own_weights, (((1,), (1,)), ((), ())), preferred_element_type=F32)
    pre_all = pre_all.reshape(n_dp * n_ex, slab, 3 * part)
    hidden_a, _, gate_a, up_a = activations(pre_all[:, :CAP], pre_all[:, CAP:], part)
    top = jnp.concatenate([gate_a, up_a, jnp.zeros_like(hidden_a)], axis=2)
    bottom = jnp.concatenate([jnp.zeros_like(gate_a), jnp.zeros_like(up_a), hidden_a], axis=2)
    factors = jnp.concatenate([top, bottom], axis=1).reshape(-1, 3 * part)
    weight_grad = lax.dot_general(factors, every, (((0,), (0,)), ((), ())), preferred_element_type=F32)
    weight_grad = jnp.transpose(weight_grad.reshape(3, part, width), (1, 0, 2))

    back = back.reshape(n_ex * slab, half)
    input_grad = jnp.concatenate(
        [
            lax.dot_general(p, back, (((0,), (0,)), ((), ())), preferred_element_type=F32).astype(BF16)
            for p in (pick_tok16, pick_cot16)
        ],
        axis=1,
    )
    route_te = jnp.sum(jnp.where(pick_tok[:, :CAP], back_route[:, :, None], 0.0), axis=1).T
    route_grad = (
        jnp.sum(jnp.where(chosen, route_te[:, None, :], 0.0), axis=2) / scale16
    ).astype(BF16)
    return (input_grad, route_grad, weight_grad[None])


def solution(mesh):
    in_specs = (
        P(("dp", "expert"), None),
        P(("dp", "expert"), None),
        P(("dp", "expert"), None),
        P(("dp", "expert"), None),
        P("expert", None, None, None),
    )
    out_specs = (
        P(("dp", "expert"), None),
        P(("dp", "expert"), None),
        P("expert", "dp", None, None),
    )
    return jax.shard_map(shards, mesh=mesh, in_specs=in_specs, out_specs=out_specs, check_vma=False)
```

```python
import functools

import jax
import jax.numpy as jnp
from jax import lax
from jax.experimental import pallas as pl
from jax.experimental.pallas import tpu as pltpu
from jax.sharding import PartitionSpec as P

CAP = 36
MESH = pl.DeviceIdType.MESH
F32 = jnp.float32
BF16 = jnp.bfloat16


def dispatch_kernel(
    n_dp, n_ex, send_ref, out_ref, self_sem, s_ex, r_ex, s_mate, r_mate, s_y, r_y, s_fwd, r_fwd
):
    d, e = lax.axis_index("dp"), lax.axis_index("expert")
    n_y, half = n_dp // 2, n_ex // 2
    y, core = d // 2, lax.rem(d, 2)
    mate = d + 1 - 2 * core
    side, place = e // half, lax.rem(e, half)

    def y_peer(j):
        return lax.rem(y + j, n_y) * 2 + core

    barrier = pltpu.get_barrier_semaphore()
    for k in range(1, n_ex):
        pl.semaphore_signal(barrier, inc=1, device_id=(d, lax.rem(e + k, n_ex)), device_id_type=MESH)
    for j in range(1, n_y):
        pl.semaphore_signal(barrier, inc=1, device_id=(y_peer(j), e), device_id_type=MESH)
    pl.semaphore_signal(barrier, inc=1, device_id=(mate, e), device_id_type=MESH)
    pl.semaphore_wait(barrier, n_ex - 1 + n_y - 1 + 1)

    cols = send_ref.shape[2] // 2

    def across(far):
        return (1 - side) * half if far else side * half

    def to_expert(far, r, h):
        dest = across(far) + lax.rem(place + r, half)
        piece = pl.ds(h * cols, cols)
        return pltpu.make_async_remote_copy(
            src_ref=send_ref.at[dest, :, piece], dst_ref=out_ref.at[d, e, :, piece],
            send_sem=s_ex.at[far, r, h], recv_sem=r_ex.at[far, r, h], device_id=(d, dest), device_id_type=MESH)

    def source(far, r):
        return across(far) + lax.rem(place + half - r, half)

    def from_expert(far, r, h):
        src = source(far, r)
        piece = pl.ds(h * cols, cols)
        return pltpu.make_async_remote_copy(
            src_ref=send_ref.at[src, :, piece], dst_ref=out_ref.at[d, src, :, piece],
            send_sem=s_ex.at[far, r, h], recv_sem=r_ex.at[far, r, h], device_id=(d, src), device_id_type=MESH)

    def move(group, far, r, h, to, send_sem, recv_sem):
        slab = out_ref.at[group, source(far, r), :, pl.ds(h * cols, cols)]
        return pltpu.make_async_remote_copy(
            src_ref=slab, dst_ref=slab, send_sem=send_sem, recv_sem=recv_sem, device_id=(to, e),
            device_id_type=MESH)

    def to_mate(group, far, r, h):
        return move(group, far, r, h, mate, s_mate.at[far, r, h], r_mate.at[far, r, h])

    def to_y(group, far, r, h, j):
        return move(group, far, r, h, y_peer(j), s_y.at[j, far, r, h], r_y.at[j, far, r, h])

    def pass_on(group, far, r, h, j):
        return move(group, far, r, h, mate, s_fwd.at[j, far, r, h], r_fwd.at[j, far, r, h])

    def y_source(j):
        return lax.rem(y + n_y - j, n_y) * 2

    pending = []

    def forward(far, r, h):
        if far or r:
            from_expert(far, r, h).wait_recv()
        for j in range(1, n_y):
            to_y(d, far, r, h, j).start()
        to_mate(d, far, r, h).start()
        pending.append((far, r, h))

    def relay(lag):
        while len(pending) > lag:
            flow = pending.pop(0)
            for j in range(1, n_y):
                to_y(y_source(j) + core, *flow, j).wait_recv()
                pass_on(y_source(j) + core, *flow, j).start()

    own = pltpu.make_async_copy(send_ref.at[e], out_ref.at[d, e], self_sem)
    own.start()
    far_flows = [(1, r, h) for r in range(half) for h in (0, 1)]
    near_flows = [(0, r, h) for r in range(1, half) for h in (0, 1)]
    for p, flow in enumerate(far_flows):
        if p >= 2:
            to_expert(*far_flows[p - 2]).wait_send()
        to_expert(*flow).start()
        if p < len(near_flows):
            to_expert(*near_flows[p]).start()
        if p == 0:
            own.wait()
            forward(0, 0, 0)
            forward(0, 0, 1)
        if p >= 2:
            forward(*far_flows[p - 2])
        if 1 <= p <= len(near_flows):
            forward(*near_flows[p - 1])
        relay(6)
    forward(*far_flows[-2])
    relay(3)
    forward(*far_flows[-1])
    relay(0)
    flows = [(far, r, h) for r in range(half) for far in (0, 1) for h in (0, 1)]
    for flow in flows:
        to_mate(mate, *flow).wait_recv()
        for j in range(1, n_y):
            pass_on(y_source(j) + 1 - core, *flow, j).wait_recv()
    to_expert(*far_flows[-2]).wait_send()
    to_expert(*far_flows[-1]).wait_send()
    for flow in near_flows:
        to_expert(*flow).wait_send()
    for flow in flows:
        to_mate(d, *flow).wait_send()
        for j in range(1, n_y):
            to_y(d, *flow, j).wait_send()
            pass_on(y_source(j) + core, *flow, j).wait_send()


def dispatch(send, n_dp, n_ex):
    _, rows, width = send.shape
    n_y, half = n_dp // 2, n_ex // 2
    dma = pltpu.SemaphoreType.DMA
    return pl.pallas_call(
        functools.partial(dispatch_kernel, n_dp, n_ex),
        out_shape=jax.ShapeDtypeStruct((n_dp, n_ex, rows, width), send.dtype),
        in_specs=[pl.BlockSpec(memory_space=pl.ANY)],
        out_specs=pl.BlockSpec(memory_space=pl.ANY),
        scratch_shapes=[dma] + [dma((2, half, 2))] * 4 + [dma((n_y, 2, half, 2))] * 4,
        compiler_params=pltpu.CompilerParams(collective_id=0, has_side_effects=True),
    )(send)


def activations(pre_tok, pre_cot, hid):
    gate_pre, up_pre = pre_tok[..., :hid], pre_tok[..., hid : 2 * hid]
    grad_hidden = pre_cot[..., 2 * hid :]
    logistic = jax.nn.sigmoid(gate_pre)
    hidden = (gate_pre * logistic * up_pre).astype(BF16)
    gate_delta = (grad_hidden * up_pre * logistic * (1.0 + gate_pre * (1.0 - logistic))).astype(BF16)
    up_delta = (grad_hidden * gate_pre * logistic).astype(BF16)
    return hidden, grad_hidden, gate_delta, up_delta


def shards(tokens, cotangent, expert_ids, route_weights, expert_weights):
    n_ex, n_dp = lax.axis_size("expert"), lax.axis_size("dp")
    tok_rows, width = tokens.shape
    hid = expert_weights.shape[1]
    part = hid // n_dp
    slab = 2 * CAP
    half = width // 2

    columns = jnp.arange(n_ex, dtype=jnp.int32)
    chosen = expert_ids[:, :, None] == columns
    member = jnp.any(chosen, axis=1)
    scale16 = route_weights.astype(BF16).astype(F32)
    scale_te = jnp.sum(jnp.where(chosen, scale16[:, :, None], 0.0), axis=1)
    lower = (jnp.arange(tok_rows)[:, None] > jnp.arange(tok_rows)[None, :]).astype(BF16)
    slot_te = jnp.dot(lower, member.astype(BF16), preferred_element_type=F32).astype(jnp.int32)
    slot = jnp.where(member, slot_te, -1).T
    lanes = jnp.arange(slab, dtype=jnp.int32)[None, :, None]
    pick_tok = (slot[:, None, :] == lanes)
    pick_cot = (slot[:, None, :] == lanes - CAP) & (lanes >= CAP)
    pick_tok = pick_tok & (lanes < CAP)
    row_scale = jnp.sum(jnp.where(pick_cot, scale_te.T[:, None, :], 0.0), axis=2).reshape(-1, 1)
    pick_tok16 = pick_tok.astype(BF16).reshape(-1, tok_rows)
    pick_cot16 = pick_cot.astype(BF16).reshape(-1, tok_rows)
    send = (
        jnp.dot(pick_tok16, tokens, preferred_element_type=F32)
        + row_scale * jnp.dot(pick_cot16, cotangent, preferred_element_type=F32)
    ).astype(BF16)

    rows = dispatch(send.reshape(n_ex, slab, width), n_dp, n_ex)
    d = lax.axis_index("dp")
    weights = jnp.transpose(expert_weights[0], (1, 0, 2))
    flat_weights = weights.reshape(3 * hid, width)

    mine = lax.dynamic_index_in_dim(rows, d, 0, keepdims=False).reshape(n_ex * slab, width)
    pre = lax.dot_general(mine, flat_weights, (((1,), (1,)), ((), ())), preferred_element_type=F32)
    pre = pre.reshape(n_ex, slab, 3 * hid)
    hidden, grad_hidden, gate_delta, up_delta = activations(pre[:, :CAP], pre[:, CAP:], hid)
    route_rows = jnp.sum(hidden.astype(F32) * grad_hidden, axis=2)
    deltas = jnp.concatenate([gate_delta, up_delta], axis=2)
    nothing = jnp.zeros_like(deltas)
    left = jnp.concatenate([deltas, nothing], axis=1).reshape(n_ex * slab, 2 * hid)
    right = jnp.concatenate([nothing, deltas], axis=1).reshape(n_ex * slab, 2 * hid)
    input_rows = (
        jnp.dot(left, flat_weights[: 2 * hid, :half], preferred_element_type=F32)
        + jnp.dot(right, flat_weights[: 2 * hid, half:], preferred_element_type=F32)
    ).astype(BF16)
    all_route = lax.all_gather(route_rows, "expert", axis=0, tiled=False)
    all_route, input_rows, rows = lax.optimization_barrier((all_route, input_rows, rows))
    back_route = lax.dynamic_index_in_dim(all_route, lax.axis_index("expert"), 1, keepdims=False)
    back = lax.all_to_all(
        input_rows.reshape(n_ex, slab, half), "expert", split_axis=0, concat_axis=0, tiled=True
    )

    own_weights = lax.dynamic_slice_in_dim(weights, d * part, part, axis=1).reshape(3 * part, width)
    every = rows.reshape(n_dp * n_ex * slab, width)
    pre_all = lax.dot_general(every, own_weights, (((1,), (1,)), ((), ())), preferred_element_type=F32)
    pre_all = pre_all.reshape(n_dp * n_ex, slab, 3 * part)
    hidden_a, _, gate_a, up_a = activations(pre_all[:, :CAP], pre_all[:, CAP:], part)
    top = jnp.concatenate([gate_a, up_a, jnp.zeros_like(hidden_a)], axis=2)
    bottom = jnp.concatenate([jnp.zeros_like(gate_a), jnp.zeros_like(up_a), hidden_a], axis=2)
    factors = jnp.concatenate([top, bottom], axis=1).reshape(-1, 3 * part)
    weight_grad = lax.dot_general(factors, every, (((0,), (0,)), ((), ())), preferred_element_type=F32)
    weight_grad = jnp.transpose(weight_grad.reshape(3, part, width), (1, 0, 2))

    back = back.reshape(n_ex * slab, half)
    input_grad = jnp.concatenate(
        [
            lax.dot_general(p, back, (((0,), (0,)), ((), ())), preferred_element_type=F32).astype(BF16)
            for p in (pick_tok16, pick_cot16)
        ],
        axis=1,
    )
    route_te = jnp.sum(jnp.where(pick_tok[:, :CAP], back_route[:, :, None], 0.0), axis=1).T
    route_grad = (
        jnp.sum(jnp.where(chosen, route_te[:, None, :], 0.0), axis=2) / scale16
    ).astype(BF16)
    return (input_grad, route_grad, weight_grad[None])


def solution(mesh):
    in_specs = (
        P(("dp", "expert"), None),
        P(("dp", "expert"), None),
        P(("dp", "expert"), None),
        P(("dp", "expert"), None),
        P("expert", None, None, None),
    )
    out_specs = (
        P(("dp", "expert"), None),
        P(("dp", "expert"), None),
        P("expert", "dp", None, None),
    )
    return jax.shard_map(shards, mesh=mesh, in_specs=in_specs, out_specs=out_specs, check_vma=False)
```
